512 devices in a mesh: res: 64 (over y, z_lo, core), ch: 8 (over z_hi, x).
Axes of the slice: x: 4, y: 4, z: 16 (z_hi: 2, z_lo: 8; z = z_hi * 8 + z_lo), core: 2. Of those that a mesh axis runs over, the one named last changes fastest.
Arguments:
- pair_rep: bfloat16 [512, 512, 128], P('res', 'ch'), may hold values from -6 to 6
- pair_mask: int32 [512, 512], P('res', 'ch'), may hold values from 0 to 1, as said below
- norm_gain: float32 [128], replicated, may hold values from 0.1 to 1.9
- norm_bias: float32 [128], replicated, may hold values from -2.5 to 2.5
- left_proj: bfloat16 [128, 128], replicated, may hold values from -0.5 to 0.5
- left_gate: bfloat16 [128, 128], replicated, may hold values from -0.5 to 0.5
- right_proj: bfloat16 [128, 128], replicated, may hold values from -0.5 to 0.5
- right_gate: bfloat16 [128, 128], replicated, may hold values from -0.5 to 0.5
- gate_proj: bfloat16 [128, 128], replicated, may hold values from -0.5 to 0.5
- out_gain: float32 [128], replicated, may hold values from 0.1 to 1.9
- out_bias: float32 [128], replicated, may hold values from -2.5 to 2.5
- out_proj: bfloat16 [128, 128], replicated, may hold values from -0.5 to 0.5
Outputs:
- update: bfloat16 [512, 512, 128], P('res', 'ch')
The draws below stay inside these ranges and needn't reach their ends.
Inputs may be any that keep to these rules, and one draw needn't show every extreme that they name: pair_mask[i, j] = v[i] v[j] for a 0/1 vector v over the 512 tokens; v is 0 for trailing padding after a length L between 384 and 448, and also for scattered unresolved tokens before L.
All inputs are finite; a program needn't handle non-finite values.
Results may differ from the reference program's by a relative error of at most 0.017.
Values may be sent and summed in bfloat16 or wider, within the bound.
No kernel may reach another device: no remote copies, remote signals or barrier semaphores. Data moves between devices by JAX's collectives and lax.ppermute only.
A program may use at most 64 MiB of HBM per device.

```python
import jax
import jax.numpy as jnp
from jax import lax

TOKENS = 512
C = 128
H = 128


def draw_pair_mask(key, part):
    key = jax.random.fold_in(key, 7)
    length_key, hole_key = jax.random.split(key)
    length = jax.random.randint(length_key, (), TOKENS - TOKENS // 4, TOKENS - TOKENS // 8 + 1)
    resolved = jax.random.randint(hole_key, (TOKENS,), 0, 8) != 0
    valid = ((jnp.arange(TOKENS) < length) & resolved).astype(jnp.int32)
    return valid[:, None] * valid[None, :]


def block_scale(rng, shape, shards, smallest, largest):
    level = 1.0
    for axis_at, shards_of in shards:
        steps = jax.random.uniform(jax.random.fold_in(jax.random.fold_in(rng, 6), axis_at), (shards_of,), jnp.float32, smallest / len(shards), largest / len(shards))
        level = level * jnp.repeat(jnp.exp(steps), shape[axis_at] // shards_of).reshape((-1,) + (1,) * (len(shape) - 1 - axis_at))
    return level


def noise(key, shape, scale, most, cuts=(), dtype=jnp.bfloat16):
    result = jax.random.normal(key, shape, jnp.float32) * scale
    if len(cuts) > 0:
        result = block_scale(key, shape, cuts, -0.22, 0.18) * result
    return jnp.clip(result, min=-most, max=most).astype(dtype)


def setup_inputs(seed: int = 0) -> dict:
    key_list = jax.random.split(jax.random.key(seed), 13)
    return {
        "pair_rep": noise(key_list[0], (TOKENS, TOKENS, C), 1.0, 6.0, ((0, 64), (1, 8))),
        "pair_mask": draw_pair_mask(jax.random.fold_in(key_list[12], 71), 0),
        "norm_gain": jnp.clip(1.0 + 0.18 * jax.random.normal(key_list[2], (C,), jnp.float32), 0.1, 1.9),
        "norm_bias": noise(key_list[3], (C,), 0.5, 2.5, (), jnp.float32),
        "left_proj": noise(key_list[4], (C, H), C ** -0.5, 0.5),
        "left_gate": noise(key_list[5], (C, H), C ** -0.5, 0.5),
        "right_proj": noise(key_list[6], (C, H), C ** -0.5, 0.5),
        "right_gate": noise(key_list[7], (C, H), C ** -0.5, 0.5),
        "gate_proj": noise(key_list[8], (C, C), C ** -0.5, 0.5),
        "out_gain": jnp.clip(1.0 + 0.18 * jax.random.normal(key_list[9], (H,), jnp.float32), 0.1, 1.9),
        "out_bias": noise(key_list[10], (H,), 0.5, 2.5, (), jnp.float32),
        "out_proj": noise(key_list[11], (H, C), H ** -0.5, 0.5),
    }


def layer_norm(values, gain, bias):
    mean = lax.optimization_barrier(jnp.mean(values, axis=-1, keepdims=True))
    centred = values - mean
    spread = lax.optimization_barrier(jnp.mean(centred * centred, axis=-1, keepdims=True))
    return centred * lax.rsqrt(spread + 1e-05) * gain + bias

def reference(pair_rep, pair_mask, norm_gain, norm_bias, left_proj, left_gate, right_proj, right_gate, gate_proj, out_gain, out_bias, out_proj):
    count = pair_rep.shape[0]
    width = pair_rep.shape[2]
    normed = layer_norm(pair_rep.astype(jnp.float32), norm_gain, norm_bias).astype(jnp.bfloat16)
    flat = normed.reshape(count * count, width)
    maskf = pair_mask.astype(jnp.float32).reshape(count * count, 1)

    def project(weight):
        return jnp.dot(flat, weight, preferred_element_type=jnp.float32)
    left = (maskf * jax.nn.sigmoid(project(left_gate)) * project(left_proj)).astype(jnp.bfloat16)
    right = (maskf * jax.nn.sigmoid(project(right_gate)) * project(right_proj)).astype(jnp.bfloat16)
    hidden = left.shape[1]
    left = left.reshape(count, count, hidden).astype(jnp.float32)
    right = right.reshape(count, count, hidden).astype(jnp.float32)
    mixed = jnp.einsum('ikc,jkc->ijc', left, right)
    mixed_norm = layer_norm(mixed, out_gain, out_bias).astype(jnp.bfloat16)
    projected = jnp.dot(mixed_norm.reshape(count * count, hidden), out_proj, preferred_element_type=jnp.float32)
    gating = jax.nn.sigmoid(project(gate_proj))
    return (gating * projected).astype(jnp.bfloat16).reshape(count, count, width)
```

```python
import jax
import jax.numpy as jnp
from jax import lax
from jax.experimental import pallas as pl
from jax.experimental.pallas import tpu as pltpu
from jax.sharding import Mesh
from jax.sharding import PartitionSpec as P

EPS = 1e-05
F32, BF16 = jnp.float32, jnp.bfloat16
VMEM_LIMIT = 32 * 1024 * 1024


def dot_last(a, b):
    return lax.dot_general(a, b, (((1,), (1,)), ((), ())), preferred_element_type=F32)


def call(kernel, outs, scratch, *args, flops=1 << 24):
    return pl.pallas_call(
        kernel,
        out_shape=outs,
        scratch_shapes=scratch,
        compiler_params=pltpu.CompilerParams(vmem_limit_bytes=VMEM_LIMIT),
    )(*args)


def prepare(x_ref, mask_ref, gain_ref, bias_ref, lp_ref, lg_ref, rp_ref, rg_ref, gate_ref, send_ref, gating_ref, rows):
    x = x_ref[...].astype(F32)
    mean = jnp.mean(x, axis=-1, keepdims=True)
    centred = x - mean
    spread = jnp.mean(centred * centred, axis=-1, keepdims=True)
    normed = (centred * lax.rsqrt(spread + EPS) * gain_ref[...] + bias_ref[...]).astype(BF16)

    def edge(proj_ref, gate_ref):
        value = dot_last(proj_ref[...].T, normed)
        gate = dot_last(gate_ref[...].T, normed)
        return jax.nn.sigmoid(gate) * value

    left = edge(lp_ref, lg_ref)
    right = edge(rp_ref, rg_ref)
    mask = mask_ref[...].astype(F32)
    mask = jnp.concatenate([mask, mask], axis=1)
    for i in range(8):
        at = slice(i * 64, (i + 1) * 64)
        both = jnp.concatenate([left[:, at], right[:, at]], axis=1)
        rows[:, i, :] = both * mask[i : i + 1, :]
    send_ref[...] = rows[...].reshape(1024, 128).astype(BF16)
    gating_ref[...] = jax.nn.sigmoid(jnp.dot(normed, gate_ref[...], preferred_element_type=F32))


def contract(own_ref, both_ref, send_ref, lhs, out):
    own = own_ref[...].astype(F32).reshape(32, 4, 8, 128)
    both = both_ref[...].astype(F32).reshape(2, 32, 4, 8, 128)
    for x in range(2):
        lhs[x] = jnp.concatenate([own[:, 2 * x, :, :64], own[:, 2 * x + 1, :, :64]], axis=-1).reshape(256, 128)
    parts = []
    for x in range(4):
        part = jnp.stack([both[0, :, x], both[1, :, x]], axis=1).reshape(512, 128)
        parts.append(part[:, 64:])
    rhs = jnp.concatenate(parts, axis=1).astype(BF16)
    mixed = []
    for e in range(2):
        halves = [lhs[x, pl.ds(e, 128, stride=2), :] for x in range(2)]
        mixed.append(dot_last(jnp.concatenate(halves, axis=1).astype(BF16), rhs))
    for h in range(8):
        at = slice(h * 64, (h + 1) * 64)
        tile = jnp.concatenate([mixed[0][:, at], mixed[1][:, at]], axis=1).reshape(16, 8, 128)
        out[:, 0, h * 4 : (h + 1) * 4, :] = tile[:, 0:4, :]
        out[:, 1, h * 4 : (h + 1) * 4, :] = tile[:, 4:8, :]
    send_ref[...] = out[...].reshape(1024, 128).astype(BF16)


def finish(got_ref, gating_ref, gain_ref, bias_ref, proj_ref, out_ref, rows):
    got = got_ref[...].astype(F32).reshape(32, 2, 16, 128)
    rows[...] = (got[:, 0] + got[:, 1]).reshape(512, 128)
    gain = jnp.broadcast_to(gain_ref[...], (128, 128)).T
    bias = jnp.broadcast_to(bias_ref[...], (128, 128)).T
    for a in range(4):
        mixed = rows[pl.ds(a, 128, stride=4), :]
        mean = jnp.mean(mixed, axis=0, keepdims=True)
        centred = mixed - mean
        spread = jnp.mean(centred * centred, axis=0, keepdims=True)
        normed = (centred * lax.rsqrt(spread + EPS) * gain + bias).astype(BF16)
        projected = lax.dot_general(normed, proj_ref[...], (((0,), (0,)), ((), ())), preferred_element_type=F32)
        at = slice(a * 128, (a + 1) * 128)
        out_ref[at, :] = (gating_ref[at, :] * projected).astype(BF16)


def on_device(
    pair_rep,
    pair_mask,
    norm_gain,
    norm_bias,
    left_proj,
    left_gate,
    right_proj,
    right_gate,
    gate_proj,
    out_gain,
    out_bias,
    out_proj,
):
    send, gating = call(
        prepare,
        (jax.ShapeDtypeStruct((1024, 128), BF16), jax.ShapeDtypeStruct((512, 128), F32)),
        [pltpu.VMEM((128, 8, 128), F32)],
        pair_rep.reshape(512, 128),
        pair_mask,
        norm_gain.reshape(1, 128),
        norm_bias.reshape(1, 128),
        left_proj,
        left_gate,
        right_proj,
        right_gate,
        gate_proj,
    )
    got = lax.all_to_all(send.reshape(128, 8, 128), ("y", "z_lo", "x"), 0, 0, tiled=True).reshape(1024, 128)
    both = lax.all_gather(got, "core", axis=0, tiled=True)
    send = call(
        contract,
        jax.ShapeDtypeStruct((1024, 128), BF16),
        [pltpu.VMEM((2, 256, 128), F32), pltpu.VMEM((16, 2, 32, 128), F32)],
        got,
        both,
    )
    got = lax.all_to_all(send.reshape(256, 4, 128), ("y", "z_lo", "z_hi", "x"), 0, 0, tiled=True).reshape(1024, 128)
    out = call(
        finish,
        jax.ShapeDtypeStruct((512, 128), BF16),
        [pltpu.VMEM((512, 128), F32)],
        got,
        gating,
        out_gain.reshape(1, 128),
        out_bias.reshape(1, 128),
        out_proj,
    )
    return out.reshape(8, 64, 128)


def solution(mesh):
    fine = Mesh(mesh.devices.reshape(4, 8, 2, 2, 4), ("y", "z_lo", "core", "z_hi", "x"))
    res, ch = ("y", "z_lo", "core"), ("z_hi", "x")
    placed = (P(res, ch, None), P(res, ch)) + (P(),) * 10
    return jax.shard_map(on_device, mesh=fine, in_specs=placed, out_specs=P(res, ch, None), check_vma=False)
```

```python
import jax
import jax.numpy as jnp
from jax import lax
from jax.experimental import pallas as pl
from jax.experimental.pallas import tpu as pltpu
from jax.sharding import Mesh
from jax.sharding import PartitionSpec as P

EPS = 1e-05
F32, BF16 = jnp.float32, jnp.bfloat16
VMEM_LIMIT = 32 * 1024 * 1024


def dot_last(a, b):
    return lax.dot_general(a, b, (((1,), (1,)), ((), ())), preferred_element_type=F32)


def call(kernel, outs, scratch, *args, space=pltpu.VMEM, limit=VMEM_LIMIT):
    return pl.pallas_call(
        kernel,
        out_shape=outs,
        in_specs=[pl.BlockSpec(memory_space=space)] * len(args),
        scratch_shapes=scratch,
        compiler_params=pltpu.CompilerParams(vmem_limit_bytes=limit),
    )(*args)


def prepare(*refs):
    sources, (send_ref, gating_ref, affine_ref, last_ref, rows), held, sems = refs[:12], refs[12:17], refs[17:29], refs[29]
    copies = [pltpu.make_async_copy(s, h, sems.at[n]) for n, (s, h) in enumerate(zip(sources, held))]
    for copy in copies:
        copy.start()
    x_ref, mask_ref, gain_ref, bias_ref, lp_ref, lg_ref, rp_ref, rg_ref, gate_ref, og_ref, ob_ref, op_ref = held
    copies[0].wait()
    x = x_ref[...].astype(F32)
    mean = jnp.mean(x, axis=-1, keepdims=True)
    centred = x - mean
    spread = jnp.mean(centred * centred, axis=-1, keepdims=True)
    scaled = centred * lax.rsqrt(spread + EPS)
    for copy in copies[1:]:
        copy.wait()
    normed = (scaled * gain_ref[...] + bias_ref[...]).astype(BF16)

    def edge(proj_ref, gate_ref):
        value = dot_last(proj_ref[...].T, normed)
        gate = dot_last(gate_ref[...].T, normed)
        return jax.nn.sigmoid(gate) * value

    left = edge(lp_ref, lg_ref)
    right = edge(rp_ref, rg_ref)
    mask = mask_ref[...].astype(F32)
    mask = jnp.concatenate([mask, mask], axis=1)
    for i in range(8):
        at = slice(i * 64, (i + 1) * 64)
        both = jnp.concatenate([left[:, at], right[:, at]], axis=1)
        rows[:, i, :] = both * mask[i : i + 1, :]
    send_ref[...] = rows[...].reshape(1024, 128).astype(BF16)
    gating_ref[...] = jax.nn.sigmoid(jnp.dot(normed, gate_ref[...], preferred_element_type=F32))
    affine_ref[0] = jnp.broadcast_to(og_ref[...], (128, 128)).T
    affine_ref[1] = jnp.broadcast_to(ob_ref[...], (128, 128)).T
    last_ref[...] = op_ref[...]


def contract(own_ref, both_ref, send_ref, lhs, out):
    own = own_ref[...].astype(F32).reshape(32, 4, 8, 128)
    both = both_ref[...].astype(F32).reshape(2, 32, 4, 8, 128)
    for x in range(2):
        lhs[x] = jnp.concatenate([own[:, 2 * x, :, :64], own[:, 2 * x + 1, :, :64]], axis=-1).reshape(256, 128)
    parts = []
    for x in range(4):
        part = jnp.stack([both[0, :, x], both[1, :, x]], axis=1).reshape(512, 128)
        parts.append(part[:, 64:])
    rhs = jnp.concatenate(parts, axis=1).astype(BF16)
    mixed = []
    for e in range(2):
        halves = [lhs[x, pl.ds(e, 128, stride=2), :] for x in range(2)]
        mixed.append(dot_last(jnp.concatenate(halves, axis=1).astype(BF16), rhs))
    for h in range(8):
        at = slice(h * 64, (h + 1) * 64)
        tile = jnp.concatenate([mixed[0][:, at], mixed[1][:, at]], axis=1).reshape(16, 8, 128)
        out[:, 0, h * 4 : (h + 1) * 4, :] = tile[:, 0:4, :]
        out[:, 1, h * 4 : (h + 1) * 4, :] = tile[:, 4:8, :]
    send_ref[...] = out[...].reshape(1024, 128).astype(BF16)


def finish(got_ref, gating_ref, affine_ref, proj_ref, out_ref, rows):
    got = got_ref[...].astype(F32).reshape(32, 2, 16, 128)
    rows[...] = (got[:, 0] + got[:, 1]).reshape(512, 128)
    for a in range(4):
        mixed = rows[pl.ds(a, 128, stride=4), :]
        mean = jnp.mean(mixed, axis=0, keepdims=True)
        centred = mixed - mean
        spread = jnp.mean(centred * centred, axis=0, keepdims=True)
        normed = (centred * lax.rsqrt(spread + EPS) * affine_ref[0] + affine_ref[1]).astype(BF16)
        projected = lax.dot_general(normed, proj_ref[...], (((0,), (0,)), ((), ())), preferred_element_type=F32)
        at = slice(a * 128, (a + 1) * 128)
        out_ref[at, :] = (gating_ref[at, :] * projected).astype(BF16)


def on_device(
    pair_rep,
    pair_mask,
    norm_gain,
    norm_bias,
    left_proj,
    left_gate,
    right_proj,
    right_gate,
    gate_proj,
    out_gain,
    out_bias,
    out_proj,
):
    operands = (
        pair_rep.reshape(512, 128),
        pair_mask,
        norm_gain.reshape(1, 128),
        norm_bias.reshape(1, 128),
        left_proj,
        left_gate,
        right_proj,
        right_gate,
        gate_proj,
        out_gain.reshape(1, 128),
        out_bias.reshape(1, 128),
        out_proj,
    )
    send, gating, affine, last = call(
        prepare,
        (
            jax.ShapeDtypeStruct((1024, 128), BF16),
            jax.ShapeDtypeStruct((512, 128), F32),
            jax.ShapeDtypeStruct((2, 128, 128), F32),
            jax.ShapeDtypeStruct((128, 128), BF16),
        ),
        [pltpu.VMEM((128, 8, 128), F32)]
        + [pltpu.VMEM(o.shape, o.dtype) for o in operands]
        + [pltpu.SemaphoreType.DMA((len(operands),))],
        *operands,
        space=pltpu.HBM,
        limit=64 * 1024 * 1024 - 512 * 1024,
    )
    got = lax.all_to_all(send.reshape(128, 8, 128), ("y", "z_lo", "x"), 0, 0, tiled=True).reshape(1024, 128)
    both = lax.all_gather(got, "core", axis=0, tiled=True)
    send = call(
        contract,
        jax.ShapeDtypeStruct((1024, 128), BF16),
        [pltpu.VMEM((2, 256, 128), F32), pltpu.VMEM((16, 2, 32, 128), F32)],
        got,
        both,
    )
    got = lax.all_to_all(send.reshape(256, 4, 128), ("y", "z_lo", "z_hi", "x"), 0, 0, tiled=True).reshape(1024, 128)
    out = call(
        finish,
        jax.ShapeDtypeStruct((512, 128), BF16),
        [pltpu.VMEM((512, 128), F32)],
        got,
        gating,
        affine,
        last,
    )
    return out.reshape(8, 64, 128)


def solution(mesh):
    fine = Mesh(mesh.devices.reshape(4, 8, 2, 2, 4), ("y", "z_lo", "core", "z_hi", "x"))
    res, ch = ("y", "z_lo", "core"), ("z_hi", "x")
    placed = (P(res, ch, None), P(res, ch)) + (P(),) * 10
    return jax.shard_map(on_device, mesh=fine, in_specs=placed, out_specs=P(res, ch, None), check_vma=False)
```

```python
import jax
import jax.numpy as jnp
from jax import lax
from jax.experimental import pallas as pl
from jax.experimental.pallas import tpu as pltpu
from jax.sharding import Mesh
from jax.sharding import PartitionSpec as P

EPS = 1e-05
F32, BF16 = jnp.float32, jnp.bfloat16
VMEM_LIMIT = 32 * 1024 * 1024


def dot_last(a, b):
    return lax.dot_general(a, b, (((1,), (1,)), ((), ())), preferred_element_type=F32)


def call(kernel, outs, scratch, *args, space=pltpu.VMEM, limit=VMEM_LIMIT):
    return pl.pallas_call(
        kernel,
        out_shape=outs,
        in_specs=[pl.BlockSpec(memory_space=space)] * len(args),
        scratch_shapes=scratch,
        compiler_params=pltpu.CompilerParams(vmem_limit_bytes=limit),
    )(*args)


def prepare(*refs):
    sources, (send_ref, gating_ref, affine_ref, last_ref, rows), held, sems = refs[:12], refs[12:17], refs[17:29], refs[29]
    copies = [pltpu.make_async_copy(s, h, sems.at[n]) for n, (s, h) in enumerate(zip(sources, held))]
    for copy in copies:
        copy.start()
    x_ref, mask_ref, gain_ref, bias_ref, lp_ref, lg_ref, rp_ref, rg_ref, gate_ref, og_ref, ob_ref, op_ref = held
    copies[0].wait()
    x = x_ref[...].astype(F32)
    mean = jnp.mean(x, axis=-1, keepdims=True)
    centred = x - mean
    spread = jnp.mean(centred * centred, axis=-1, keepdims=True)
    scaled = centred * lax.rsqrt(spread + EPS)
    for copy in copies[1:]:
        copy.wait()
    normed = (scaled * gain_ref[...] + bias_ref[...]).astype(BF16)

    def edge(proj_ref, gate_ref):
        value = dot_last(proj_ref[...].T, normed)
        gate = dot_last(gate_ref[...].T, normed)
        return jax.nn.sigmoid(gate) * value

    left = edge(lp_ref, lg_ref)
    right = edge(rp_ref, rg_ref)
    mask = mask_ref[...].astype(F32)
    mask = jnp.concatenate([mask, mask], axis=1)
    for i in range(8):
        at = slice(i * 64, (i + 1) * 64)
        both = jnp.concatenate([left[:, at], right[:, at]], axis=1)
        rows[:, i, :] = both * mask[i : i + 1, :]
    send_ref[...] = rows[...].reshape(1024, 128).astype(BF16)
    gating_ref[...] = jax.nn.sigmoid(jnp.dot(normed, gate_ref[...], preferred_element_type=F32))
    affine_ref[0] = jnp.broadcast_to(og_ref[...], (128, 128)).T
    affine_ref[1] = jnp.broadcast_to(ob_ref[...], (128, 128)).T
    last_ref[...] = op_ref[...]


def contract(own_ref, both_ref, send_ref, lhs, out):
    own = own_ref[...].astype(F32).reshape(4, 4, 64, 128)
    both = both_ref[...].astype(F32).reshape(2, 4, 4, 8, 8, 128)
    for x in range(2):
        lhs[x] = jnp.concatenate([own[:, 2 * x, :, :64], own[:, 2 * x + 1, :, :64]], axis=-1).reshape(256, 128)
    parts = []
    for x in range(4):
        part = jnp.stack([both[0, :, x], both[1, :, x]], axis=2).reshape(512, 128)
        parts.append(part[:, 64:])
    rhs = jnp.concatenate(parts, axis=1).astype(BF16)
    mixed = []
    for e in range(2):
        halves = [lhs[x, pl.ds(e, 128, stride=2), :] for x in range(2)]
        mixed.append(dot_last(jnp.concatenate(halves, axis=1).astype(BF16), rhs))
    for h in range(8):
        at = slice(h * 64, (h + 1) * 64)
        tile = jnp.concatenate([mixed[0][:, at], mixed[1][:, at]], axis=1).reshape(4, 4, 8, 128)
        to = slice(h % 4 * 4, h % 4 * 4 + 4)
        for y in range(4):
            for s in range(2):
                out[:, s, h // 4, y, to, :] = tile[y, :, 4 * s : 4 * s + 4, :]
    send_ref[...] = out[...].reshape(1024, 128).astype(BF16)


def add_halves(got_ref, send_ref, out):
    got = got_ref[...].astype(F32).reshape(8, 2, 64, 128)
    for z in range(8):
        total = (got[z, 0] + got[z, 1]).reshape(8, 8, 128)
        for s in range(2):
            out[:, s, z * 4 : z * 4 + 4, :] = total[:, 4 * s : 4 * s + 4, :]
    send_ref[...] = out[...].reshape(512, 128).astype(BF16)


def finish(got_ref, gating_ref, affine_ref, proj_ref, out_ref, rows):
    rows[...] = got_ref[...].astype(F32)
    for a in range(4):
        mixed = rows[pl.ds(a, 128, stride=4), :]
        mean = jnp.mean(mixed, axis=0, keepdims=True)
        centred = mixed - mean
        spread = jnp.mean(centred * centred, axis=0, keepdims=True)
        normed = (centred * lax.rsqrt(spread + EPS) * affine_ref[0] + affine_ref[1]).astype(BF16)
        projected = lax.dot_general(normed, proj_ref[...], (((0,), (0,)), ((), ())), preferred_element_type=F32)
        at = slice(a * 128, (a + 1) * 128)
        out_ref[at, :] = (gating_ref[at, :] * projected).astype(BF16)


def on_device(
    pair_rep,
    pair_mask,
    norm_gain,
    norm_bias,
    left_proj,
    left_gate,
    right_proj,
    right_gate,
    gate_proj,
    out_gain,
    out_bias,
    out_proj,
):
    operands = (
        pair_rep.reshape(512, 128),
        pair_mask,
        norm_gain.reshape(1, 128),
        norm_bias.reshape(1, 128),
        left_proj,
        left_gate,
        right_proj,
        right_gate,
        gate_proj,
        out_gain.reshape(1, 128),
        out_bias.reshape(1, 128),
        out_proj,
    )
    send, gating, affine, last = call(
        prepare,
        (
            jax.ShapeDtypeStruct((1024, 128), BF16),
            jax.ShapeDtypeStruct((512, 128), F32),
            jax.ShapeDtypeStruct((2, 128, 128), F32),
            jax.ShapeDtypeStruct((128, 128), BF16),
        ),
        [pltpu.VMEM((128, 8, 128), F32)]
        + [pltpu.VMEM(o.shape, o.dtype) for o in operands]
        + [pltpu.SemaphoreType.DMA((len(operands),))],
        *operands,
        space=pltpu.HBM,
        limit=64 * 1024 * 1024 - 512 * 1024,
    )
    got = lax.all_to_all(send.reshape(128, 8, 128), ("y", "x", "z_lo"), 0, 0, tiled=True).reshape(1024, 128)
    both = lax.all_gather(got, "core", axis=0, tiled=True)
    send = call(
        contract,
        jax.ShapeDtypeStruct((1024, 128), BF16),
        [pltpu.VMEM((2, 256, 128), F32), pltpu.VMEM((4, 2, 2, 4, 16, 128), F32)],
        got,
        both,
    )
    got = lax.all_to_all(send.reshape(16, 64, 128), ("z_lo", "z_hi"), 0, 0, tiled=True).reshape(1024, 128)
    send = call(
        add_halves,
        jax.ShapeDtypeStruct((512, 128), BF16),
        [pltpu.VMEM((8, 2, 32, 128), F32)],
        got,
    )
    got = lax.all_to_all(send.reshape(16, 32, 128), ("y", "x"), 0, 0, tiled=True).reshape(512, 128)
    out = call(
        finish,
        jax.ShapeDtypeStruct((512, 128), BF16),
        [pltpu.VMEM((512, 128), F32)],
        got,
        gating,
        affine,
        last,
    )
    return out.reshape(8, 64, 128)


def solution(mesh):
    fine = Mesh(mesh.devices.reshape(4, 8, 2, 2, 4), ("y", "z_lo", "core", "z_hi", "x"))
    res, ch = ("y", "z_lo", "core"), ("z_hi", "x")
    placed = (P(res, ch, None), P(res, ch)) + (P(),) * 10
    return jax.shard_map(on_device, mesh=fine, in_specs=placed, out_specs=P(res, ch, None), check_vma=False)
```

```python
import jax
import jax.numpy as jnp
from jax import lax
from jax.experimental import pallas as pl
from jax.experimental.pallas import tpu as pltpu
from jax.sharding import Mesh
from jax.sharding import PartitionSpec as P

EPS = 1e-05
F32, BF16 = jnp.float32, jnp.bfloat16
VMEM_LIMIT = 32 * 1024 * 1024

AXES = ("y", "z_lo", "core", "z_hi", "x")
Z_IN = (3, 4, 2, 5, 1, 6, 0, 7)
Z_OUT = (8, 7, 9, 6, 10, 5, 11, 4, 12, 3, 13, 2, 14, 1, 15, 0)
AT_IN = tuple(Z_IN.index(z) for z in range(8))
AT_OUT = tuple(Z_OUT.index(z) for z in range(16))


def device(y, z, core, x):
    return (((y * 8 + z % 8) * 2 + core) * 2 + z // 8) * 4 + x


def peers(zs, core):
    return [device(y, z, core, x) for z in zs for y in range(4) for x in range(4)]


IN_GROUPS = [peers([z + 8 * half for z in Z_IN], core) for core in range(2) for half in range(2)]
OUT_GROUPS = [peers(Z_OUT, core) for core in range(2)]


def exchange(rows, groups):
    count = len(groups[0])
    chunks = rows.reshape(count, rows.shape[0] // count, 128)
    return lax.all_to_all(chunks, AXES, 0, 0, axis_index_groups=groups, tiled=True).reshape(rows.shape)


def dot_last(a, b):
    return lax.dot_general(a, b, (((1,), (1,)), ((), ())), preferred_element_type=F32)


def call(kernel, outs, scratch, *args, space=pltpu.VMEM, limit=VMEM_LIMIT):
    return pl.pallas_call(
        kernel,
        out_shape=outs,
        in_specs=[pl.BlockSpec(memory_space=space)] * len(args),
        scratch_shapes=scratch,
        compiler_params=pltpu.CompilerParams(vmem_limit_bytes=limit),
    )(*args)


def prepare(*refs):
    sources, (send_ref, gating_ref, affine_ref, last_ref, rows), held, sems = refs[:12], refs[12:17], refs[17:29], refs[29]
    copies = [pltpu.make_async_copy(s, h, sems.at[n]) for n, (s, h) in enumerate(zip(sources, held))]
    for copy in copies:
        copy.start()
    x_ref, mask_ref, gain_ref, bias_ref, lp_ref, lg_ref, rp_ref, rg_ref, gate_ref, og_ref, ob_ref, op_ref = held
    copies[0].wait()
    x = x_ref[...].astype(F32)
    mean = jnp.mean(x, axis=-1, keepdims=True)
    centred = x - mean
    spread = jnp.mean(centred * centred, axis=-1, keepdims=True)
    scaled = centred * lax.rsqrt(spread + EPS)
    for copy in copies[1:]:
        copy.wait()
    normed = (scaled * gain_ref[...] + bias_ref[...]).astype(BF16)

    def edge(proj_ref, gate_ref):
        value = dot_last(proj_ref[...].T, normed)
        gate = dot_last(gate_ref[...].T, normed)
        return jax.nn.sigmoid(gate) * value

    left = edge(lp_ref, lg_ref)
    right = edge(rp_ref, rg_ref)
    mask = mask_ref[...].astype(F32)
    mask = jnp.concatenate([mask, mask], axis=1)
    for i in range(8):
        at = slice(i * 64, (i + 1) * 64)
        both = jnp.concatenate([left[:, at], right[:, at]], axis=1)
        rows[:, i, :] = both * mask[i : i + 1, :]
    send_ref[...] = rows[...].reshape(1024, 128).astype(BF16)
    gating_ref[...] = jax.nn.sigmoid(jnp.dot(normed, gate_ref[...], preferred_element_type=F32))
    affine_ref[0] = jnp.broadcast_to(og_ref[...], (128, 128)).T
    affine_ref[1] = jnp.broadcast_to(ob_ref[...], (128, 128)).T
    last_ref[...] = op_ref[...]


def contract(own_ref, both_ref, send_ref, lhs, out):
    own = own_ref[...].astype(F32).reshape(32, 4, 8, 128)
    both = both_ref[...].astype(F32).reshape(2, 8, 4, 4, 8, 128)
    for x in range(2):
        lhs[x] = jnp.concatenate([own[:, 2 * x, :, :64], own[:, 2 * x + 1, :, :64]], axis=-1).reshape(256, 128)
    parts = []
    for x in range(4):
        part = [both[core, AT_IN[z], y, x] for y in range(4) for z in range(8) for core in range(2)]
        parts.append(jnp.concatenate(part, axis=0)[:, 64:])
    rhs = jnp.concatenate(parts, axis=1).astype(BF16)
    mixed = []
    for e in range(2):
        halves = [lhs[x, pl.ds(e, 128, stride=2), :] for x in range(2)]
        mixed.append(dot_last(jnp.concatenate(halves, axis=1).astype(BF16), rhs))
    for h in range(8):
        at = slice(h * 64, (h + 1) * 64)
        tile = jnp.concatenate([mixed[0][:, at], mixed[1][:, at]], axis=1).reshape(8, 2, 8, 128)
        to = slice(h % 4 * 4, h % 4 * 4 + 4)
        for place, z in enumerate(Z_IN):
            for s in range(2):
                out[AT_OUT[h // 4 * 8 + z], :, s, to, :] = tile[place, :, 4 * s : 4 * s + 4, :]
    send_ref[...] = out[...].reshape(1024, 128).astype(BF16)


def finish(got_ref, gating_ref, affine_ref, proj_ref, out_ref, rows):
    got = got_ref[...].astype(F32).reshape(16, 64, 128)
    for place, z in enumerate(Z_IN):
        rows[place * 64 : (place + 1) * 64, :] = got[AT_OUT[z]] + got[AT_OUT[z + 8]]
    for a in range(4):
        mixed = rows[pl.ds(a, 128, stride=4), :]
        mean = jnp.mean(mixed, axis=0, keepdims=True)
        centred = mixed - mean
        spread = jnp.mean(centred * centred, axis=0, keepdims=True)
        normed = (centred * lax.rsqrt(spread + EPS) * affine_ref[0] + affine_ref[1]).astype(BF16)
        projected = lax.dot_general(normed, proj_ref[...], (((0,), (0,)), ((), ())), preferred_element_type=F32)
        at = slice(a * 128, (a + 1) * 128)
        out_ref[at, :] = (gating_ref[at, :] * projected).astype(BF16)


def on_device(
    pair_rep,
    pair_mask,
    norm_gain,
    norm_bias,
    left_proj,
    left_gate,
    right_proj,
    right_gate,
    gate_proj,
    out_gain,
    out_bias,
    out_proj,
):
    operands = (
        pair_rep.reshape(512, 128),
        pair_mask,
        norm_gain.reshape(1, 128),
        norm_bias.reshape(1, 128),
        left_proj,
        left_gate,
        right_proj,
        right_gate,
        gate_proj,
        out_gain.reshape(1, 128),
        out_bias.reshape(1, 128),
        out_proj,
    )
    send, gating, affine, last = call(
        prepare,
        (
            jax.ShapeDtypeStruct((1024, 128), BF16),
            jax.ShapeDtypeStruct((512, 128), F32),
            jax.ShapeDtypeStruct((2, 128, 128), F32),
            jax.ShapeDtypeStruct((128, 128), BF16),
        ),
        [pltpu.VMEM((128, 8, 128), F32)]
        + [pltpu.VMEM(o.shape, o.dtype) for o in operands]
        + [pltpu.SemaphoreType.DMA((len(operands),))],
        *operands,
        space=pltpu.HBM,
        limit=64 * 1024 * 1024 - 512 * 1024,
    )
    got = exchange(send, IN_GROUPS)
    both = lax.all_gather(got, "core", axis=0, tiled=True)
    send = call(
        contract,
        jax.ShapeDtypeStruct((1024, 128), BF16),
        [pltpu.VMEM((2, 256, 128), F32), pltpu.VMEM((16, 2, 2, 16, 128), F32)],
        got,
        both,
    )
    got = exchange(send, OUT_GROUPS)
    out = call(
        finish,
        jax.ShapeDtypeStruct((512, 128), BF16),
        [pltpu.VMEM((512, 128), F32)],
        got,
        gating,
        affine,
        last,
    )
    return out.reshape(8, 64, 128)


def solution(mesh):
    fine = Mesh(mesh.devices.reshape(4, 8, 2, 2, 4), AXES)
    res, ch = ("y", "z_lo", "core"), ("z_hi", "x")
    placed = (P(res, ch, None), P(res, ch)) + (P(),) * 10
    return jax.shard_map(on_device, mesh=fine, in_specs=placed, out_specs=P(res, ch, None), check_vma=False)
```

```python
import jax
import jax.numpy as jnp
from jax import lax
from jax.experimental import pallas as pl
from jax.experimental.pallas import tpu as pltpu
from jax.sharding import Mesh
from jax.sharding import PartitionSpec as P

EPS = 1e-05
F32, BF16 = jnp.float32, jnp.bfloat16
VMEM_LIMIT = 32 * 1024 * 1024

AXES = ("y", "z_lo", "core", "z_hi", "x")
Z_IN = (3, 4, 2, 5, 1, 6, 0, 7)
Z_OUT = (8, 9, 7, 10, 6, 11, 5, 12, 13, 4, 14, 15, 3, 2, 1, 0)
AT_IN = tuple(Z_IN.index(z) for z in range(8))
AT_OUT = tuple(Z_OUT.index(z) for z in range(16))


def device(y, z, core, x):
    return (((y * 8 + z % 8) * 2 + core) * 2 + z // 8) * 4 + x


def peers(zs, core):
    return [device(y, z, core, x) for z in zs for y in (3, 2, 1, 0) for x in (3, 2, 1, 0)]


IN_GROUPS = [peers([z + 8 * half for z in Z_IN], core) for core in range(2) for half in range(2)]
OUT_GROUPS = [peers(Z_OUT, core) for core in range(2)]


def exchange(rows, groups):
    count = len(groups[0])
    chunks = rows.reshape(count, rows.shape[0] // count, 128)
    return lax.all_to_all(chunks, AXES, 0, 0, axis_index_groups=groups, tiled=True).reshape(rows.shape)


def dot_last(a, b):
    return lax.dot_general(a, b, (((1,), (1,)), ((), ())), preferred_element_type=F32)


def call(kernel, outs, scratch, *args, space=pltpu.VMEM, limit=VMEM_LIMIT):
    return pl.pallas_call(
        kernel,
        out_shape=outs,
        in_specs=[pl.BlockSpec(memory_space=space)] * len(args),
        scratch_shapes=scratch,
        compiler_params=pltpu.CompilerParams(vmem_limit_bytes=limit),
    )(*args)


def prepare(*refs):
    sources, (send_ref, gating_ref, affine_ref, last_ref, rows), held, sems = refs[:12], refs[12:17], refs[17:29], refs[29]
    copies = [pltpu.make_async_copy(s, h, sems.at[n]) for n, (s, h) in enumerate(zip(sources, held))]
    for copy in copies:
        copy.start()
    x_ref, mask_ref, gain_ref, bias_ref, lp_ref, lg_ref, rp_ref, rg_ref, gate_ref, og_ref, ob_ref, op_ref = held
    copies[0].wait()
    x = x_ref[...].astype(F32)
    mean = jnp.mean(x, axis=-1, keepdims=True)
    centred = x - mean
    spread = jnp.mean(centred * centred, axis=-1, keepdims=True)
    scaled = centred * lax.rsqrt(spread + EPS)
    for copy in copies[1:]:
        copy.wait()
    normed = (scaled * gain_ref[...] + bias_ref[...]).astype(BF16)

    def edge(proj_ref, gate_ref):
        value = dot_last(proj_ref[...].T, normed)
        gate = dot_last(gate_ref[...].T, normed)
        return jax.nn.sigmoid(gate) * value

    left = edge(lp_ref, lg_ref)
    right = edge(rp_ref, rg_ref)
    mask = mask_ref[...].astype(F32)
    mask = jnp.concatenate([mask, mask], axis=1)
    for i in range(8):
        at = slice(i * 64, (i + 1) * 64)
        both = jnp.concatenate([left[:, at], right[:, at]], axis=1)
        rows[:, i, :] = both * mask[i : i + 1, :]
    send_ref[...] = rows[...].reshape(1024, 128).astype(BF16)
    gating_ref[...] = jax.nn.sigmoid(jnp.dot(normed, gate_ref[...], preferred_element_type=F32))
    affine_ref[0] = jnp.broadcast_to(og_ref[...], (128, 128)).T
    affine_ref[1] = jnp.broadcast_to(ob_ref[...], (128, 128)).T
    last_ref[...] = op_ref[...]


def contract(own_ref, both_ref, send_ref, lhs, out):
    own = own_ref[...].astype(F32).reshape(32, 4, 8, 128)
    both = both_ref[...].astype(F32).reshape(2, 8, 4, 4, 8, 128)
    for x in range(2):
        lhs[x] = jnp.concatenate([own[:, 2 * x, :, :64], own[:, 2 * x + 1, :, :64]], axis=-1).reshape(256, 128)
    parts = []
    for x in range(4):
        part = [both[core, AT_IN[z], 3 - y, x] for y in range(4) for z in range(8) for core in range(2)]
        parts.append(jnp.concatenate(part, axis=0)[:, 64:])
    rhs = jnp.concatenate(parts, axis=1).astype(BF16)
    mixed = []
    for e in range(2):
        halves = [lhs[x, pl.ds(e, 128, stride=2), :] for x in range(2)]
        mixed.append(dot_last(jnp.concatenate(halves, axis=1).astype(BF16), rhs))
    for h in range(8):
        at = slice(h * 64, (h + 1) * 64)
        tile = jnp.concatenate([mixed[0][:, at], mixed[1][:, at]], axis=1).reshape(8, 2, 8, 128)
        to = slice(12 - h % 4 * 4, 16 - h % 4 * 4)
        for place, z in enumerate(Z_IN):
            for s in range(2):
                out[AT_OUT[h // 4 * 8 + z], :, s, to, :] = tile[place, :, 4 * s : 4 * s + 4, :]
    send_ref[...] = out[...].reshape(1024, 128).astype(BF16)


def finish(got_ref, gating_ref, affine_ref, proj_ref, out_ref, rows):
    got = got_ref[...].astype(F32).reshape(16, 64, 128)
    for place, z in enumerate(Z_IN):
        rows[place * 64 : (place + 1) * 64, :] = got[AT_OUT[z]] + got[AT_OUT[z + 8]]
    for a in range(4):
        mixed = rows[pl.ds(a, 128, stride=4), :]
        mean = jnp.mean(mixed, axis=0, keepdims=True)
        centred = mixed - mean
        spread = jnp.mean(centred * centred, axis=0, keepdims=True)
        normed = (centred * lax.rsqrt(spread + EPS) * affine_ref[0] + affine_ref[1]).astype(BF16)
        projected = lax.dot_general(normed, proj_ref[...], (((0,), (0,)), ((), ())), preferred_element_type=F32)
        at = slice(a * 128, (a + 1) * 128)
        out_ref[at, :] = (gating_ref[at, :] * projected).astype(BF16)


def on_device(
    pair_rep,
    pair_mask,
    norm_gain,
    norm_bias,
    left_proj,
    left_gate,
    right_proj,
    right_gate,
    gate_proj,
    out_gain,
    out_bias,
    out_proj,
):
    operands = (
        pair_rep.reshape(512, 128),
        pair_mask,
        norm_gain.reshape(1, 128),
        norm_bias.reshape(1, 128),
        left_proj,
        left_gate,
        right_proj,
        right_gate,
        gate_proj,
        out_gain.reshape(1, 128),
        out_bias.reshape(1, 128),
        out_proj,
    )
    send, gating, affine, last = call(
        prepare,
        (
            pltpu.VMEM((1024, 128), BF16),
            pltpu.VMEM((512, 128), F32),
            pltpu.VMEM((2, 128, 128), F32),
            pltpu.VMEM((128, 128), BF16),
        ),
        [pltpu.VMEM((128, 8, 128), F32)]
        + [pltpu.VMEM(o.shape, o.dtype) for o in operands]
        + [pltpu.SemaphoreType.DMA((len(operands),))],
        *[pltpu.with_memory_space_constraint(operand, pltpu.HBM) for operand in operands],
        space=pltpu.HBM,
    )
    got = exchange(send, IN_GROUPS)
    both = lax.all_gather(got, "core", axis=0, tiled=True)
    send = call(
        contract,
        jax.ShapeDtypeStruct((1024, 128), BF16),
        [pltpu.VMEM((2, 256, 128), F32), pltpu.VMEM((16, 2, 2, 16, 128), F32)],
        got,
        both,
    )
    got = exchange(send, OUT_GROUPS)
    out = call(
        finish,
        jax.ShapeDtypeStruct((512, 128), BF16),
        [pltpu.VMEM((512, 128), F32)],
        got,
        gating,
        affine,
        last,
    )
    return out.reshape(8, 64, 128)


def solution(mesh):
    fine = Mesh(mesh.devices.reshape(4, 8, 2, 2, 4), AXES)
    res, ch = ("y", "z_lo", "core"), ("z_hi", "x")
    placed = (P(res, ch, None), P(res, ch)) + (P(),) * 10
    return jax.shard_map(on_device, mesh=fine, in_specs=placed, out_specs=P(res, ch, None), check_vma=False)
```

```python
import jax
import jax.numpy as jnp
from jax import lax
from jax.experimental import pallas as pl
from jax.experimental.pallas import tpu as pltpu
from jax.sharding import Mesh
from jax.sharding import PartitionSpec as P

EPS = 1e-05
F32, BF16 = jnp.float32, jnp.bfloat16
VMEM_LIMIT = 32 * 1024 * 1024

AXES = ("y", "z_lo", "core", "z_hi", "x")
Z_IN = ((4, 3, 5, 2, 6, 1, 7, 0), (3, 4, 2, 5, 1, 6, 7, 0))
Z_OUT = (8, 9, 7, 10, 6, 11, 5, 12, 13, 4, 14, 15, 3, 2, 1, 0)
AT_IN = tuple(tuple(order.index(z) for z in range(8)) for order in Z_IN)
AT_OUT = tuple(Z_OUT.index(z) for z in range(16))


def device(y, z, core, x):
    return (((y * 8 + z % 8) * 2 + core) * 2 + z // 8) * 4 + x


def peers(zs, core):
    return [device(y, z, core, x) for z in zs for y in (3, 2, 1, 0) for x in (3, 2, 1, 0)]


IN_GROUPS = [peers([z + 8 * half for z in Z_IN[half]], core) for core in range(2) for half in range(2)]
OUT_GROUPS = [peers(Z_OUT, core) for core in range(2)]


def exchange(rows, groups):
    count = len(groups[0])
    chunks = rows.reshape(count, rows.shape[0] // count, 128)
    return lax.all_to_all(chunks, AXES, 0, 0, axis_index_groups=groups, tiled=True).reshape(rows.shape)


def dot_last(a, b):
    return lax.dot_general(a, b, (((1,), (1,)), ((), ())), preferred_element_type=F32)


def call(kernel, outs, scratch, *args, space=pltpu.VMEM, limit=VMEM_LIMIT):
    return pl.pallas_call(
        kernel,
        out_shape=outs,
        in_specs=[pl.BlockSpec(memory_space=space)] * len(args),
        scratch_shapes=scratch,
        compiler_params=pltpu.CompilerParams(vmem_limit_bytes=limit),
    )(*args)


def prepare(*refs):
    sources, (send_ref, gating_ref, affine_ref, last_ref, rows), held, sems = refs[:12], refs[12:17], refs[17:29], refs[29]
    copies = [pltpu.make_async_copy(s, h, sems.at[n]) for n, (s, h) in enumerate(zip(sources, held))]
    for copy in copies:
        copy.start()
    x_ref, mask_ref, gain_ref, bias_ref, lp_ref, lg_ref, rp_ref, rg_ref, gate_ref, og_ref, ob_ref, op_ref = held
    copies[0].wait()
    x = x_ref[...].astype(F32)
    mean = jnp.mean(x, axis=-1, keepdims=True)
    centred = x - mean
    spread = jnp.mean(centred * centred, axis=-1, keepdims=True)
    scaled = centred * lax.rsqrt(spread + EPS)
    for copy in copies[1:]:
        copy.wait()
    normed = (scaled * gain_ref[...] + bias_ref[...]).astype(BF16)

    def edge(proj_ref, gate_ref):
        value = dot_last(proj_ref[...].T, normed)
        gate = dot_last(gate_ref[...].T, normed)
        return jax.nn.sigmoid(gate) * value

    left = edge(lp_ref, lg_ref)
    right = edge(rp_ref, rg_ref)
    mask = mask_ref[...].astype(F32)
    mask = jnp.concatenate([mask, mask], axis=1)
    for i in range(8):
        at = slice(i * 64, (i + 1) * 64)
        both = jnp.concatenate([left[:, at], right[:, at]], axis=1)
        rows[:, i, :] = both * mask[i : i + 1, :]
    send_ref[...] = rows[...].reshape(1024, 128).astype(BF16)
    gating_ref[...] = jax.nn.sigmoid(jnp.dot(normed, gate_ref[...], preferred_element_type=F32))
    affine_ref[0] = jnp.broadcast_to(og_ref[...], (128, 128)).T
    affine_ref[1] = jnp.broadcast_to(ob_ref[...], (128, 128)).T
    last_ref[...] = op_ref[...]


def contract(own_ref, both_ref, send_ref, lhs, out):
    half = lax.axis_index("z_hi")

    def block(ref, core, z):
        place = jnp.where(half == 0, AT_IN[0][z], AT_IN[1][z])
        at = pl.multiple_of(core * 1024 + place * 128, 128)
        return ref[pl.ds(at, 128), :].astype(F32).reshape(4, 4, 8, 128)

    for z in range(8):
        own = block(own_ref, 0, z)
        for x in range(2):
            pair = jnp.concatenate([own[:, 2 * x, :, :64], own[:, 2 * x + 1, :, :64]], axis=-1)
            lhs[x, z * 32 : (z + 1) * 32, :] = pair.reshape(32, 128)
    both = [[block(both_ref, core, z) for z in range(8)] for core in range(2)]
    parts = []
    for x in range(4):
        part = [both[core][z][3 - y, x] for y in range(4) for z in range(8) for core in range(2)]
        parts.append(jnp.concatenate(part, axis=0)[:, 64:])
    rhs = jnp.concatenate(parts, axis=1).astype(BF16)
    mixed = []
    for e in range(2):
        halves = [lhs[x, pl.ds(e, 128, stride=2), :] for x in range(2)]
        mixed.append(dot_last(jnp.concatenate(halves, axis=1).astype(BF16), rhs))
    for h in range(8):
        at = slice(h * 64, (h + 1) * 64)
        tile = jnp.concatenate([mixed[0][:, at], mixed[1][:, at]], axis=1).reshape(8, 2, 8, 128)
        to = slice(12 - h % 4 * 4, 16 - h % 4 * 4)
        for z in range(8):
            for s in range(2):
                out[AT_OUT[h // 4 * 8 + z], :, s, to, :] = tile[z, :, 4 * s : 4 * s + 4, :]
    send_ref[...] = out[...].reshape(1024, 128).astype(BF16)


def finish(got_ref, gating_ref, affine_ref, proj_ref, out_ref, rows):
    got = got_ref[...].astype(F32).reshape(16, 64, 128)
    for place in range(8):
        low, high = Z_IN[0][place], Z_IN[1][place] + 8
        rows[place * 64 : (place + 1) * 64, :] = got[AT_OUT[low]] + got[AT_OUT[high]]
    for a in range(4):
        mixed = rows[pl.ds(a, 128, stride=4), :]
        mean = jnp.mean(mixed, axis=0, keepdims=True)
        centred = mixed - mean
        spread = jnp.mean(centred * centred, axis=0, keepdims=True)
        normed = (centred * lax.rsqrt(spread + EPS) * affine_ref[0] + affine_ref[1]).astype(BF16)
        projected = lax.dot_general(normed, proj_ref[...], (((0,), (0,)), ((), ())), preferred_element_type=F32)
        at = slice(a * 128, (a + 1) * 128)
        out_ref[at, :] = (gating_ref[at, :] * projected).astype(BF16)


def on_device(
    pair_rep,
    pair_mask,
    norm_gain,
    norm_bias,
    left_proj,
    left_gate,
    right_proj,
    right_gate,
    gate_proj,
    out_gain,
    out_bias,
    out_proj,
):
    operands = (
        pair_rep.reshape(512, 128),
        pair_mask,
        norm_gain.reshape(1, 128),
        norm_bias.reshape(1, 128),
        left_proj,
        left_gate,
        right_proj,
        right_gate,
        gate_proj,
        out_gain.reshape(1, 128),
        out_bias.reshape(1, 128),
        out_proj,
    )
    send, gating, affine, last = call(
        prepare,
        (
            pltpu.VMEM((1024, 128), BF16),
            pltpu.VMEM((512, 128), F32),
            pltpu.VMEM((2, 128, 128), F32),
            pltpu.VMEM((128, 128), BF16),
        ),
        [pltpu.VMEM((128, 8, 128), F32)]
        + [pltpu.VMEM(o.shape, o.dtype) for o in operands]
        + [pltpu.SemaphoreType.DMA((len(operands),))],
        *[pltpu.with_memory_space_constraint(operand, pltpu.HBM) for operand in operands],
        space=pltpu.HBM,
    )
    got = exchange(send, IN_GROUPS)
    both = lax.all_gather(got, "core", axis=0, tiled=True)
    send = call(
        contract,
        jax.ShapeDtypeStruct((1024, 128), BF16),
        [pltpu.VMEM((2, 256, 128), F32), pltpu.VMEM((16, 2, 2, 16, 128), F32)],
        got,
        both,
    )
    got = exchange(send, OUT_GROUPS)
    out = call(
        finish,
        jax.ShapeDtypeStruct((512, 128), BF16),
        [pltpu.VMEM((512, 128), F32)],
        got,
        gating,
        affine,
        last,
    )
    return out.reshape(8, 64, 128)


def solution(mesh):
    fine = Mesh(mesh.devices.reshape(4, 8, 2, 2, 4), AXES)
    res, ch = ("y", "z_lo", "core"), ("z_hi", "x")
    placed = (P(res, ch, None), P(res, ch)) + (P(),) * 10
    return jax.shard_map(on_device, mesh=fine, in_specs=placed, out_specs=P(res, ch, None), check_vma=False)
```

```python
import jax
import jax.numpy as jnp
from jax import lax
from jax.experimental import pallas as pl
from jax.experimental.pallas import tpu as pltpu
from jax.sharding import Mesh
from jax.sharding import PartitionSpec as P

EPS = 1e-05
F32, BF16 = jnp.float32, jnp.bfloat16
VMEM_LIMIT = 32 * 1024 * 1024

AXES = ("y", "z_lo", "core", "z_hi", "x")
Z_IN = ((5, 4, 3, 6, 2, 1, 7, 0), (3, 4, 2, 5, 6, 1, 7, 0))
Z_OUT = (8, 9, 7, 10, 6, 11, 5, 12, 13, 4, 14, 15, 3, 2, 1, 0)
AT_IN = tuple(tuple(order.index(z) for z in range(8)) for order in Z_IN)
AT_OUT = tuple(Z_OUT.index(z) for z in range(16))


def device(y, z, core, x):
    return (((y * 8 + z % 8) * 2 + core) * 2 + z // 8) * 4 + x


def peers(zs, core):
    return [device(y, z, core, x) for z in zs for y in (3, 2, 1, 0) for x in (3, 2, 1, 0)]


IN_GROUPS = [peers([z + 8 * half for z in Z_IN[half]], core) for core in range(2) for half in range(2)]
OUT_GROUPS = [peers(Z_OUT, core) for core in range(2)]


def exchange(rows, groups):
    count = len(groups[0])
    chunks = rows.reshape(count, rows.shape[0] // count, 128)
    return lax.all_to_all(chunks, AXES, 0, 0, axis_index_groups=groups, tiled=True).reshape(rows.shape)


def dot_last(a, b):
    return lax.dot_general(a, b, (((1,), (1,)), ((), ())), preferred_element_type=F32)


def call(kernel, outs, scratch, *args, space=pltpu.VMEM, limit=VMEM_LIMIT):
    return pl.pallas_call(
        kernel,
        out_shape=outs,
        in_specs=[pl.BlockSpec(memory_space=space)] * len(args),
        scratch_shapes=scratch,
        compiler_params=pltpu.CompilerParams(vmem_limit_bytes=limit),
    )(*args)


def prepare(*refs):
    sources, (send_ref, gating_ref, affine_ref, last_ref, rows), held, sems = refs[:12], refs[12:17], refs[17:29], refs[29]
    copies = [pltpu.make_async_copy(s, h, sems.at[n]) for n, (s, h) in enumerate(zip(sources, held))]
    for copy in copies:
        copy.start()
    x_ref, mask_ref, gain_ref, bias_ref, lp_ref, lg_ref, rp_ref, rg_ref, gate_ref, og_ref, ob_ref, op_ref = held
    copies[0].wait()
    x = x_ref[...].astype(F32)
    mean = jnp.mean(x, axis=-1, keepdims=True)
    centred = x - mean
    spread = jnp.mean(centred * centred, axis=-1, keepdims=True)
    scaled = centred * lax.rsqrt(spread + EPS)
    for copy in copies[1:]:
        copy.wait()
    normed = (scaled * gain_ref[...] + bias_ref[...]).astype(BF16)

    def edge(proj_ref, gate_ref):
        value = dot_last(proj_ref[...].T, normed)
        gate = dot_last(gate_ref[...].T, normed)
        return jax.nn.sigmoid(gate) * value

    left = edge(lp_ref, lg_ref)
    right = edge(rp_ref, rg_ref)
    mask = mask_ref[...].astype(F32)
    mask = jnp.concatenate([mask, mask], axis=1)
    for i in range(8):
        at = slice(i * 64, (i + 1) * 64)
        both = jnp.concatenate([left[:, at], right[:, at]], axis=1)
        rows[:, i, :] = both * mask[i : i + 1, :]
    send_ref[...] = rows[...].reshape(1024, 128).astype(BF16)
    gating_ref[...] = jax.nn.sigmoid(jnp.dot(normed, gate_ref[...], preferred_element_type=F32))
    affine_ref[0] = jnp.broadcast_to(og_ref[...], (128, 128)).T
    affine_ref[1] = jnp.broadcast_to(ob_ref[...], (128, 128)).T
    last_ref[...] = op_ref[...]


def contract(own_ref, both_ref, send_ref, lhs, out):
    half = lax.axis_index("z_hi")

    def block(ref, core, z):
        place = jnp.where(half == 0, AT_IN[0][z], AT_IN[1][z])
        at = pl.multiple_of(core * 1024 + place * 128, 128)
        return ref[pl.ds(at, 128), :].astype(F32).reshape(4, 4, 8, 128)

    for z in range(8):
        own = block(own_ref, 0, z)
        for x in range(2):
            pair = jnp.concatenate([own[:, 2 * x, :, :64], own[:, 2 * x + 1, :, :64]], axis=-1)
            lhs[x, z * 32 : (z + 1) * 32, :] = pair.reshape(32, 128)
    both = [[block(both_ref, core, z) for z in range(8)] for core in range(2)]
    parts = []
    for x in range(4):
        part = [both[core][z][3 - y, x] for y in range(4) for z in range(8) for core in range(2)]
        parts.append(jnp.concatenate(part, axis=0)[:, 64:])
    rhs = jnp.concatenate(parts, axis=1).astype(BF16)
    mixed = []
    for e in range(2):
        halves = [lhs[x, pl.ds(e, 128, stride=2), :] for x in range(2)]
        mixed.append(dot_last(jnp.concatenate(halves, axis=1).astype(BF16), rhs))
    for h in range(8):
        at = slice(h * 64, (h + 1) * 64)
        tile = jnp.concatenate([mixed[0][:, at], mixed[1][:, at]], axis=1).reshape(8, 2, 8, 128)
        to = slice(12 - h % 4 * 4, 16 - h % 4 * 4)
        for z in range(8):
            for s in range(2):
                out[AT_OUT[h // 4 * 8 + z], :, s, to, :] = tile[z, :, 4 * s : 4 * s + 4, :]
    send_ref[...] = out[...].reshape(1024, 128).astype(BF16)


def finish(got_ref, gating_ref, affine_ref, proj_ref, out_ref, rows):
    got = got_ref[...].astype(F32).reshape(16, 64, 128)
    for place in range(8):
        low, high = Z_IN[0][place], Z_IN[1][place] + 8
        rows[place * 64 : (place + 1) * 64, :] = got[AT_OUT[low]] + got[AT_OUT[high]]
    for a in range(4):
        mixed = rows[pl.ds(a, 128, stride=4), :]
        mean = jnp.mean(mixed, axis=0, keepdims=True)
        centred = mixed - mean
        spread = jnp.mean(centred * centred, axis=0, keepdims=True)
        normed = (centred * lax.rsqrt(spread + EPS) * affine_ref[0] + affine_ref[1]).astype(BF16)
        projected = lax.dot_general(normed, proj_ref[...], (((0,), (0,)), ((), ())), preferred_element_type=F32)
        at = slice(a * 128, (a + 1) * 128)
        out_ref[at, :] = (gating_ref[at, :] * projected).astype(BF16)


def on_device(
    pair_rep,
    pair_mask,
    norm_gain,
    norm_bias,
    left_proj,
    left_gate,
    right_proj,
    right_gate,
    gate_proj,
    out_gain,
    out_bias,
    out_proj,
):
    operands = (
        pair_rep.reshape(512, 128),
        pair_mask,
        norm_gain.reshape(1, 128),
        norm_bias.reshape(1, 128),
        left_proj,
        left_gate,
        right_proj,
        right_gate,
        gate_proj,
        out_gain.reshape(1, 128),
        out_bias.reshape(1, 128),
        out_proj,
    )
    send, gating, affine, last = call(
        prepare,
        (
            pltpu.VMEM((1024, 128), BF16),
            pltpu.VMEM((512, 128), F32),
            pltpu.VMEM((2, 128, 128), F32),
            pltpu.VMEM((128, 128), BF16),
        ),
        [pltpu.VMEM((128, 8, 128), F32)]
        + [pltpu.VMEM(o.shape, o.dtype) for o in operands]
        + [pltpu.SemaphoreType.DMA((len(operands),))],
        *[pltpu.with_memory_space_constraint(operand, pltpu.HBM) for operand in operands],
        space=pltpu.HBM,
    )
    got = exchange(send, IN_GROUPS)
    both = lax.all_gather(got, "core", axis=0, tiled=True)
    send = call(
        contract,
        jax.ShapeDtypeStruct((1024, 128), BF16),
        [pltpu.VMEM((2, 256, 128), F32), pltpu.VMEM((16, 2, 2, 16, 128), F32)],
        got,
        both,
    )
    got = exchange(send, OUT_GROUPS)
    out = call(
        finish,
        jax.ShapeDtypeStruct((512, 128), BF16),
        [pltpu.VMEM((512, 128), F32)],
        got,
        gating,
        affine,
        last,
    )
    return out.reshape(8, 64, 128)


def solution(mesh):
    fine = Mesh(mesh.devices.reshape(4, 8, 2, 2, 4), AXES)
    res, ch = ("y", "z_lo", "core"), ("z_hi", "x")
    placed = (P(res, ch, None), P(res, ch)) + (P(),) * 10
    return jax.shard_map(on_device, mesh=fine, in_specs=placed, out_specs=P(res, ch, None), check_vma=False)
```

```python
import jax
import jax.numpy as jnp
from jax import lax
from jax.experimental import pallas as pl
from jax.experimental.pallas import tpu as pltpu
from jax.sharding import Mesh
from jax.sharding import PartitionSpec as P

EPS = 1e-05
F32, BF16 = jnp.float32, jnp.bfloat16
VMEM_LIMIT = 32 * 1024 * 1024

AXES = ("y", "z_lo", "core", "z_hi", "x")
Z_IN = ((4, 3, 5, 2, 6, 1, 7, 0), (3, 4, 2, 5, 1, 6, 7, 0))
Z_OUT = (8, 9, 7, 10, 6, 11, 5, 12, 13, 4, 14, 15, 3, 2, 1, 0)
AT_IN = tuple(tuple(order.index(z) for z in range(8)) for order in Z_IN)
AT_OUT = tuple(Z_OUT.index(z) for z in range(16))


def device(y, z, core, x):
    return (((y * 8 + z % 8) * 2 + core) * 2 + z // 8) * 4 + x


def peers(zs, core):
    return [device(y, z, core, x) for z in zs for y in (3, 2, 1, 0) for x in (3, 2, 1, 0)]


IN_GROUPS = [peers([z + 8 * half for z in Z_IN[half]], core) for core in range(2) for half in range(2)]
OUT_GROUPS = [peers(Z_OUT, core) for core in range(2)]


def exchange(rows, groups):
    count = len(groups[0])
    chunks = rows.reshape(count, rows.shape[0] // count, 128)
    return lax.all_to_all(chunks, AXES, 0, 0, axis_index_groups=groups, tiled=True).reshape(rows.shape)


def dot_last(a, b):
    return lax.dot_general(a, b, (((1,), (1,)), ((), ())), preferred_element_type=F32)


def call(kernel, outs, scratch, *args, space=pltpu.VMEM, limit=VMEM_LIMIT, out=None):
    return pl.pallas_call(
        kernel,
        out_shape=outs,
        in_specs=[pl.BlockSpec(memory_space=space)] * len(args),
        scratch_shapes=scratch,
        **({} if out is None else dict(out_specs=pl.BlockSpec(memory_space=out))),
        compiler_params=pltpu.CompilerParams(vmem_limit_bytes=limit),
    )(*args)


def prepare(*refs):
    sources, (send_ref, gating_ref, affine_ref, last_ref, rows), held, sems = refs[:12], refs[12:17], refs[17:29], refs[29]
    copies = [pltpu.make_async_copy(s, h, sems.at[n]) for n, (s, h) in enumerate(zip(sources, held))]
    for copy in copies:
        copy.start()
    x_ref, mask_ref, gain_ref, bias_ref, lp_ref, lg_ref, rp_ref, rg_ref, gate_ref, og_ref, ob_ref, op_ref = held
    copies[0].wait()
    x = x_ref[...].astype(F32)
    mean = jnp.mean(x, axis=-1, keepdims=True)
    centred = x - mean
    spread = jnp.mean(centred * centred, axis=-1, keepdims=True)
    scaled = centred * lax.rsqrt(spread + EPS)
    for copy in copies[1:]:
        copy.wait()
    normed = (scaled * gain_ref[...] + bias_ref[...]).astype(BF16)

    def edge(proj_ref, gate_ref):
        value = dot_last(proj_ref[...].T, normed)
        gate = dot_last(gate_ref[...].T, normed)
        return jax.nn.sigmoid(gate) * value

    left = edge(lp_ref, lg_ref)
    right = edge(rp_ref, rg_ref)
    mask = mask_ref[...].astype(F32)
    mask = jnp.concatenate([mask, mask], axis=1)
    for i in range(8):
        at = slice(i * 64, (i + 1) * 64)
        both = jnp.concatenate([left[:, at], right[:, at]], axis=1)
        rows[:, i, :] = both * mask[i : i + 1, :]
    send_ref[...] = rows[...].reshape(1024, 128).astype(BF16)
    gating_ref[...] = jax.nn.sigmoid(jnp.dot(normed, gate_ref[...], preferred_element_type=F32))
    affine_ref[0] = jnp.broadcast_to(og_ref[...], (128, 128)).T
    affine_ref[1] = jnp.broadcast_to(ob_ref[...], (128, 128)).T
    last_ref[...] = op_ref[...]


def contract(own_ref, both_ref, send_ref, lhs, out):
    half = lax.axis_index("z_hi")

    def block(ref, core, z):
        place = jnp.where(half == 0, AT_IN[0][z], AT_IN[1][z])
        at = pl.multiple_of(core * 1024 + place * 128, 128)
        return ref[pl.ds(at, 128), :].astype(F32).reshape(4, 4, 8, 128)

    for z in range(8):
        own = block(own_ref, 0, z)
        for x in range(2):
            pair = jnp.concatenate([own[:, 2 * x, :, :64], own[:, 2 * x + 1, :, :64]], axis=-1)
            lhs[x, z * 32 : (z + 1) * 32, :] = pair.reshape(32, 128)
    both = [[block(both_ref, core, z) for z in range(8)] for core in range(2)]
    parts = []
    for x in range(4):
        part = [both[core][z][3 - y, x] for y in range(4) for z in range(8) for core in range(2)]
        parts.append(jnp.concatenate(part, axis=0)[:, 64:])
    rhs = jnp.concatenate(parts, axis=1).astype(BF16)
    mixed = []
    for e in range(2):
        halves = [lhs[x, pl.ds(e, 128, stride=2), :] for x in range(2)]
        mixed.append(dot_last(jnp.concatenate(halves, axis=1).astype(BF16), rhs))
    for h in range(8):
        at = slice(h * 64, (h + 1) * 64)
        tile = jnp.concatenate([mixed[0][:, at], mixed[1][:, at]], axis=1).reshape(8, 2, 8, 128)
        to = slice(12 - h % 4 * 4, 16 - h % 4 * 4)
        for z in range(8):
            for s in range(2):
                out[AT_OUT[h // 4 * 8 + z], :, s, to, :] = tile[z, :, 4 * s : 4 * s + 4, :]
    send_ref[...] = out[...].reshape(1024, 128).astype(BF16)


def finish(got_ref, gating_ref, affine_ref, proj_ref, out_ref, rows, done, sems):
    got = got_ref[...].astype(F32).reshape(16, 64, 128)
    for place in range(8):
        low, high = Z_IN[0][place], Z_IN[1][place] + 8
        rows[place * 64 : (place + 1) * 64, :] = got[AT_OUT[low]] + got[AT_OUT[high]]
    copies = []
    for a in range(4):
        mixed = rows[pl.ds(a, 128, stride=4), :]
        mean = jnp.mean(mixed, axis=0, keepdims=True)
        centred = mixed - mean
        spread = jnp.mean(centred * centred, axis=0, keepdims=True)
        normed = (centred * lax.rsqrt(spread + EPS) * affine_ref[0] + affine_ref[1]).astype(BF16)
        projected = lax.dot_general(normed, proj_ref[...], (((0,), (0,)), ((), ())), preferred_element_type=F32)
        at = pl.ds(a * 128, 128)
        done[at, :] = (gating_ref[at, :] * projected).astype(BF16)
        copies.append(pltpu.make_async_copy(done.at[at, :], out_ref.at[at, :], sems.at[a]))
        copies[-1].start()
    for copy in copies:
        copy.wait()


def on_device(
    pair_rep,
    pair_mask,
    norm_gain,
    norm_bias,
    left_proj,
    left_gate,
    right_proj,
    right_gate,
    gate_proj,
    out_gain,
    out_bias,
    out_proj,
):
    operands = (
        pair_rep.reshape(512, 128),
        pair_mask,
        norm_gain.reshape(1, 128),
        norm_bias.reshape(1, 128),
        left_proj,
        left_gate,
        right_proj,
        right_gate,
        gate_proj,
        out_gain.reshape(1, 128),
        out_bias.reshape(1, 128),
        out_proj,
    )
    send, gating, affine, last = call(
        prepare,
        (
            pltpu.VMEM((1024, 128), BF16),
            pltpu.VMEM((512, 128), F32),
            pltpu.VMEM((2, 128, 128), F32),
            pltpu.VMEM((128, 128), BF16),
        ),
        [pltpu.VMEM((128, 8, 128), F32)]
        + [pltpu.VMEM(o.shape, o.dtype) for o in operands]
        + [pltpu.SemaphoreType.DMA((len(operands),))],
        *[pltpu.with_memory_space_constraint(operand, pltpu.HBM) for operand in operands],
        space=pltpu.HBM,
    )
    got = exchange(send, IN_GROUPS)
    both = lax.all_gather(got, "core", axis=0, tiled=True)
    send = call(
        contract,
        jax.ShapeDtypeStruct((1024, 128), BF16),
        [pltpu.VMEM((2, 256, 128), F32), pltpu.VMEM((16, 2, 2, 16, 128), F32)],
        got,
        both,
    )
    got = exchange(send, OUT_GROUPS)
    out = call(
        finish,
        jax.ShapeDtypeStruct((512, 128), BF16),
        [pltpu.VMEM((512, 128), F32), pltpu.VMEM((512, 128), BF16), pltpu.SemaphoreType.DMA((4,))],
        got,
        gating,
        affine,
        last,
        out=pltpu.HBM,
    )
    return out.reshape(8, 64, 128)


def solution(mesh):
    fine = Mesh(mesh.devices.reshape(4, 8, 2, 2, 4), AXES)
    res, ch = ("y", "z_lo", "core"), ("z_hi", "x")
    placed = (P(res, ch, None), P(res, ch)) + (P(),) * 10
    return jax.shard_map(on_device, mesh=fine, in_specs=placed, out_specs=P(res, ch, None), check_vma=False)
```

```python
import jax
import jax.numpy as jnp
from jax import lax
from jax.experimental import pallas as pl
from jax.experimental.pallas import tpu as pltpu
from jax.sharding import Mesh
from jax.sharding import PartitionSpec as P

EPS = 1e-05
F32, BF16 = jnp.float32, jnp.bfloat16
VMEM_LIMIT = 32 * 1024 * 1024

AXES = ("y", "z_lo", "core", "z_hi", "x")
Z_IN = ((4, 3, 5, 2, 6, 1, 7, 0), (3, 4, 2, 5, 6, 1, 7, 0))
Z_OUT = (8, 9, 7, 10, 6, 11, 5, 12, 13, 4, 14, 15, 3, 2, 1, 0)
AT_IN = tuple(tuple(order.index(z) for z in range(8)) for order in Z_IN)
AT_OUT = tuple(Z_OUT.index(z) for z in range(16))


def device(y, z, core, x):
    return (((y * 8 + z % 8) * 2 + core) * 2 + z // 8) * 4 + x


def peers(zs, core):
    return [device(y, z, core, x) for z in zs for y in (3, 2, 1, 0) for x in (3, 2, 1, 0)]


IN_GROUPS = [peers([z + 8 * half for z in Z_IN[half]], core) for core in range(2) for half in range(2)]
OUT_GROUPS = [peers(Z_OUT, core) for core in range(2)]


def exchange(rows, groups):
    count = len(groups[0])
    chunks = rows.reshape(count, rows.shape[0] // count, 128)
    return lax.all_to_all(chunks, AXES, 0, 0, axis_index_groups=groups, tiled=True).reshape(rows.shape)


def dot_last(a, b):
    return lax.dot_general(a, b, (((1,), (1,)), ((), ())), preferred_element_type=F32)


def call(kernel, outs, scratch, *args, space=pltpu.VMEM, limit=VMEM_LIMIT):
    return pl.pallas_call(
        kernel,
        out_shape=outs,
        in_specs=[pl.BlockSpec(memory_space=space)] * len(args),
        scratch_shapes=scratch,
        compiler_params=pltpu.CompilerParams(vmem_limit_bytes=limit),
    )(*args)


def prepare(*refs):
    sources, (send_ref, gating_ref, affine_ref, last_ref, rows), held, sems = refs[:12], refs[12:17], refs[17:29], refs[29]
    copies = [pltpu.make_async_copy(s, h, sems.at[n]) for n, (s, h) in enumerate(zip(sources, held))]
    for copy in copies:
        copy.start()
    x_ref, mask_ref, gain_ref, bias_ref, lp_ref, lg_ref, rp_ref, rg_ref, gate_ref, og_ref, ob_ref, op_ref = held
    copies[0].wait()
    x = x_ref[...].astype(F32)
    mean = jnp.mean(x, axis=-1, keepdims=True)
    centred = x - mean
    spread = jnp.mean(centred * centred, axis=-1, keepdims=True)
    scaled = centred * lax.rsqrt(spread + EPS)
    for copy in copies[1:]:
        copy.wait()
    normed = (scaled * gain_ref[...] + bias_ref[...]).astype(BF16)

    def edge(proj_ref, gate_ref):
        value = dot_last(proj_ref[...].T, normed)
        gate = dot_last(gate_ref[...].T, normed)
        return jax.nn.sigmoid(gate) * value

    left = edge(lp_ref, lg_ref)
    right = edge(rp_ref, rg_ref)
    mask = mask_ref[...].astype(F32)
    mask = jnp.concatenate([mask, mask], axis=1)
    for i in range(8):
        at = slice(i * 64, (i + 1) * 64)
        both = jnp.concatenate([left[:, at], right[:, at]], axis=1)
        rows[:, i, :] = both * mask[i : i + 1, :]
    send_ref[...] = rows[...].reshape(1024, 128).astype(BF16)
    gating_ref[...] = jax.nn.sigmoid(jnp.dot(normed, gate_ref[...], preferred_element_type=F32))
    affine_ref[0] = jnp.broadcast_to(og_ref[...], (128, 128)).T
    affine_ref[1] = jnp.broadcast_to(ob_ref[...], (128, 128)).T
    last_ref[...] = op_ref[...]


def contract(own_ref, both_ref, send_ref, lhs, out):
    half = lax.axis_index("z_hi")

    def block(ref, core, z):
        place = jnp.where(half == 0, AT_IN[0][z], AT_IN[1][z])
        at = pl.multiple_of(core * 1024 + place * 128, 128)
        return ref[pl.ds(at, 128), :].astype(F32).reshape(4, 4, 8, 128)

    for z in range(8):
        own = block(own_ref, 0, z)
        for x in range(2):
            pair = jnp.concatenate([own[:, 2 * x, :, :64], own[:, 2 * x + 1, :, :64]], axis=-1)
            lhs[x, z * 32 : (z + 1) * 32, :] = pair.reshape(32, 128)
    both = [[block(both_ref, core, z) for z in range(8)] for core in range(2)]
    parts = []
    for x in range(4):
        part = [both[core][z][3 - y, x] for y in range(4) for z in range(8) for core in range(2)]
        parts.append(jnp.concatenate(part, axis=0)[:, 64:])
    rhs = jnp.concatenate(parts, axis=1).astype(BF16)
    mixed = []
    for e in range(2):
        halves = [lhs[x, pl.ds(e, 128, stride=2), :] for x in range(2)]
        mixed.append(dot_last(jnp.concatenate(halves, axis=1).astype(BF16), rhs))
    for h in range(8):
        at = slice(h * 64, (h + 1) * 64)
        tile = jnp.concatenate([mixed[0][:, at], mixed[1][:, at]], axis=1).reshape(8, 2, 8, 128)
        to = slice(12 - h % 4 * 4, 16 - h % 4 * 4)
        for z in range(8):
            for s in range(2):
                out[AT_OUT[h // 4 * 8 + z], :, s, to, :] = tile[z, :, 4 * s : 4 * s + 4, :]
    send_ref[...] = out[...].reshape(1024, 128).astype(BF16)


def finish(got_ref, gating_ref, affine_ref, proj_ref, out_ref, rows):
    got = got_ref[...].astype(F32).reshape(16, 64, 128)
    for place in range(8):
        low, high = Z_IN[0][place], Z_IN[1][place] + 8
        rows[place * 64 : (place + 1) * 64, :] = got[AT_OUT[low]] + got[AT_OUT[high]]
    for a in range(4):
        mixed = rows[pl.ds(a, 128, stride=4), :]
        mean = jnp.mean(mixed, axis=0, keepdims=True)
        centred = mixed - mean
        spread = jnp.mean(centred * centred, axis=0, keepdims=True)
        normed = (centred * lax.rsqrt(spread + EPS) * affine_ref[0] + affine_ref[1]).astype(BF16)
        projected = lax.dot_general(normed, proj_ref[...], (((0,), (0,)), ((), ())), preferred_element_type=F32)
        at = slice(a * 128, (a + 1) * 128)
        out_ref[at, :] = (gating_ref[at, :] * projected).astype(BF16)


def on_device(
    pair_rep,
    pair_mask,
    norm_gain,
    norm_bias,
    left_proj,
    left_gate,
    right_proj,
    right_gate,
    gate_proj,
    out_gain,
    out_bias,
    out_proj,
):
    operands = (
        pair_rep.reshape(512, 128),
        pair_mask,
        norm_gain.reshape(1, 128),
        norm_bias.reshape(1, 128),
        left_proj,
        left_gate,
        right_proj,
        right_gate,
        gate_proj,
        out_gain.reshape(1, 128),
        out_bias.reshape(1, 128),
        out_proj,
    )
    send, gating, affine, last = call(
        prepare,
        (
            pltpu.VMEM((1024, 128), BF16),
            pltpu.VMEM((512, 128), F32),
            pltpu.VMEM((2, 128, 128), F32),
            pltpu.VMEM((128, 128), BF16),
        ),
        [pltpu.VMEM((128, 8, 128), F32)]
        + [pltpu.VMEM(o.shape, o.dtype) for o in operands]
        + [pltpu.SemaphoreType.DMA((len(operands),))],
        *[pltpu.with_memory_space_constraint(operand, pltpu.HBM) for operand in operands],
        space=pltpu.HBM,
    )
    got = exchange(send, IN_GROUPS)
    both = lax.all_gather(got, "core", axis=0, tiled=True)
    send = call(
        contract,
        jax.ShapeDtypeStruct((1024, 128), BF16),
        [pltpu.VMEM((2, 256, 128), F32), pltpu.VMEM((16, 2, 2, 16, 128), F32)],
        got,
        both,
    )
    got = exchange(send, OUT_GROUPS)
    out = call(
        finish,
        jax.ShapeDtypeStruct((512, 128), BF16),
        [pltpu.VMEM((512, 128), F32)],
        got,
        gating,
        affine,
        last,
    )
    return out.reshape(8, 64, 128)


def solution(mesh):
    fine = Mesh(mesh.devices.reshape(4, 8, 2, 2, 4), AXES)
    res, ch = ("y", "z_lo", "core"), ("z_hi", "x")
    placed = (P(res, ch, None), P(res, ch)) + (P(),) * 10
    return jax.shard_map(on_device, mesh=fine, in_specs=placed, out_specs=P(res, ch, None), check_vma=False)
```
